32 devices in a mesh: parts: 2 (over y), region: 2 (over x), dev: 4 (over z), pair: 2 (over core).
Axes of the slice: x: 2, y: 2, z: 4, core: 2. Of those that a mesh axis runs over, the one named last changes fastest.
Arguments:
- observed_rates: bfloat16 [32, 4096], P(('parts', 'region', 'dev', 'pair')), parts along dimension 0, may hold values from -0.94921875 to 0.94921875
- block_values: bfloat16 [16, 1024, 1024], P(('parts', 'region', 'dev')), parts along dimension 0, may hold values from -0.125 to 0.125
- block_row: int32 [16], P('parts'), parts along dimension 0, may hold values from 0 to 3, as said below
- block_col: int32 [16], P('parts'), parts along dimension 0, may hold values from 0 to 3, as said below
- deal_list: int32 [16], P('parts'), parts along dimension 0, may hold values from 0 to 7, each once
- scale_index: int32 [16, 8], P(('parts', 'region', 'dev')), parts along dimension 0, may hold values from 0 to 15
- scale_table: float32 [32], P('parts'), parts along dimension 0, may hold values from 0.5 to 2
Outputs:
- errors: bfloat16 [32, 4096], P(('parts', 'region', 'dev', 'pair')), parts along dimension 0
- block_grads: bfloat16 [16, 1024, 1024], P(('parts', 'region', 'dev'), 'pair'), parts along dimension 0
The draws below stay inside these ranges and needn't reach their ends.
There are 2 independent parts, one for each index of `parts`. The reference program is written for one: setup_inputs(seed, part) draws one part's arguments, and reference() takes and returns one part's arrays. A program takes and returns all parts, laid end to end along the dimension named above; each array names one. Nothing has to cross between parts.
Inputs may be any that keep to these rules, and one draw needn't show every extreme that they name: Every block row and every block column holds exactly two blocks, and no pair (block_row, block_col) repeats. Every block column holds exactly two blocks, and no pair (block_row, block_col) repeats.
All inputs are finite; a program needn't handle non-finite values.
Results may differ from the reference program's by a relative error of at most 0.006.
Values may be sent and summed in bfloat16 or wider, within the bound.
A program may use at most 64 MiB of HBM per device.

```python
import math
import jax
import jax.numpy as jnp
from jax import lax

BLOCK = 1024
SCALES = 16
BLOCKS = 8
BROWS = 4
NEURONS = 4096
STEPS = 16
GROUPS = 8


def pattern_pairs(key):
    first_key, cycle_key, order_key = jax.random.split(key, 3)
    first = jax.random.permutation(first_key, BROWS).astype(jnp.int32)
    cycle = jax.random.permutation(cycle_key, BROWS).astype(jnp.int32)
    second = jnp.zeros((BROWS,), jnp.int32).at[cycle].set(first[jnp.roll(cycle, -1)])
    every_row = jnp.arange(BROWS, dtype=jnp.int32)
    rows_all = jnp.concatenate([every_row, every_row])
    cols_all = jnp.concatenate([first, second])
    order = jax.random.permutation(order_key, BLOCKS).astype(jnp.int32)
    return (rows_all[order], cols_all[order])


def draw_block_row(key, part):
    rows_all, cols_all = pattern_pairs(key)
    return rows_all.astype(jnp.int32)


def draw_block_col(key, part):
    rows_all, cols_all = pattern_pairs(key)
    return cols_all.astype(jnp.int32)


def with_ends(values, own_key, smallest, high):
    longest = values.shape.index(max(values.shape))
    spots = []
    for shift in (0, 1):
        where = [jax.random.randint(jax.random.fold_in(own_key, axis), (), 0, length) for axis, length in enumerate(values.shape)]
        where[longest] = (where[longest] + shift) % values.shape[longest]
        spots.append(tuple(where))
    return values.at[spots[0]].set(smallest).at[spots[1]].set(high)


def shard_levels(stream_key, dims, pieces, smallest, high):
    def one(dim, shards_of):
        draws = jax.random.uniform(jax.random.fold_in(jax.random.fold_in(stream_key, 6), dim), (shards_of,), jnp.float32, smallest / len(pieces), high / len(pieces))
        return jnp.repeat(jnp.exp(draws), dims[dim] // shards_of).reshape((-1,) + (1,) * (len(dims) - dim - 1))

    loudness = one(*pieces[0])
    for cut in pieces[1:]:
        loudness = loudness * one(*cut)
    return loudness


def gaussian(own_key, dims, deviation, bound, cuts=(), held_as=jnp.bfloat16):
    result = deviation * jax.random.normal(own_key, dims, jnp.float32)
    if cuts:
        result = result * shard_levels(own_key, dims, cuts, -0.22, 0.18)
    return jnp.clip(result, -bound, bound).astype(held_as)


def setup_inputs(seed: int = 0, part: int = 0) -> dict:
    streams_of = jax.random.split(jax.random.key(seed), 8)
    part_keys = jax.random.split(jax.random.fold_in(streams_of[7], part), 8)
    observed_rates = jnp.clip(jax.random.uniform(part_keys[0], (STEPS, NEURONS), jnp.float32, -0.94921875, 0.94921875) * shard_levels(part_keys[0], (STEPS, NEURONS), ((0, 16),), -0.4, 0.0), -0.94921875, 0.94921875).astype(jnp.bfloat16)
    block_values = gaussian(part_keys[1], (BLOCKS, BLOCK, BLOCK), (2 * BLOCK) ** -0.5, 0.125, ((0, 8),))
    block_row = draw_block_row(jax.random.fold_in(jax.random.fold_in(streams_of[7], part), 71), part)
    block_col = draw_block_col(jax.random.fold_in(jax.random.fold_in(streams_of[7], part), 71), part)
    deal_list = jax.random.permutation(part_keys[4], BLOCKS).astype(jnp.int32)
    scale_index = with_ends(jax.random.randint(part_keys[5], (BLOCKS, GROUPS), 0, SCALES), jax.random.fold_in(part_keys[5], 1), 0, SCALES - 1).astype(jnp.int32)
    scale_table = jnp.clip(jnp.exp(jax.random.uniform(part_keys[6], (SCALES,), jnp.float32, math.log(0.5), math.log(2.0))), 0.5, 2.0)
    return dict(observed_rates=observed_rates, block_values=block_values, block_row=block_row, block_col=block_col, deal_list=deal_list, scale_index=scale_index, scale_table=scale_table)


def column_scales(indices, table):
    return jnp.repeat(table[indices], 128)

def reference(observed_rates, block_values, block_row, block_col, deal_list, scale_index, scale_table):
    row_of = block_row[deal_list].astype(jnp.int32)
    col_of = block_col[deal_list].astype(jnp.int32)
    panels = observed_rates.reshape(STEPS, BROWS, BLOCK)

    def forward(currents, slot):
        column_scale = column_scales(scale_index[slot], scale_table)
        effective = (block_values[slot].astype(jnp.float32) * column_scale[None, :]).astype(jnp.bfloat16)
        source = lax.dynamic_index_in_dim(panels, col_of[slot], 1, keepdims=False)
        partial_value = lax.dot_general(source, effective, (((1,), (1,)), ((), ())), preferred_element_type=jnp.float32)
        current_row = lax.dynamic_index_in_dim(currents, row_of[slot], 1, keepdims=False)
        currents = lax.dynamic_update_index_in_dim(currents, current_row + partial_value, row_of[slot], 1)
        return (currents, None)
    start_currents = jnp.zeros((STEPS, BROWS, BLOCK), jnp.float32)
    currents, _ = lax.scan(forward, start_currents, jnp.arange(BLOCKS, dtype=jnp.int32))
    predicted = jnp.tanh(currents).reshape(STEPS, NEURONS)
    following = jnp.concatenate([observed_rates[1:], jnp.zeros((1, NEURONS), jnp.bfloat16)], axis=0)
    valid = (jnp.arange(STEPS) < STEPS - 1)[:, None]
    mismatch = jnp.where(valid, predicted - following.astype(jnp.float32), 0.0)
    errors = mismatch.astype(jnp.bfloat16)
    signal = (mismatch * (1.0 - predicted * predicted) * (1.0 / math.sqrt(STEPS))).astype(jnp.bfloat16)
    signal_panels = signal.reshape(STEPS, BROWS, BLOCK)

    def gradient(slot):
        column_scale = column_scales(scale_index[slot], scale_table)
        source = lax.dynamic_index_in_dim(panels, col_of[slot], 1, keepdims=False)
        arrived = lax.dynamic_index_in_dim(signal_panels, row_of[slot], 1, keepdims=False)
        term = lax.dot_general(arrived, source, (((0,), (0,)), ((), ())), preferred_element_type=jnp.float32)
        return (term * column_scale[None, :]).astype(jnp.bfloat16)
    block_grads = lax.map(gradient, jnp.arange(BLOCKS, dtype=jnp.int32))
    return (errors, block_grads)
```

```python
import functools
import math

import jax
import jax.numpy as jnp
from jax import lax
from jax.experimental import pallas as pl
from jax.experimental.pallas import tpu as pltpu
from jax.sharding import PartitionSpec as P

LANES = 128
MESH = pl.DeviceIdType.MESH


def repeat(count, body):
    if count <= 32:
        for i in range(count):
            body(i)
    else:
        lax.fori_loop(0, count, lambda i, carry: (body(i), carry)[1], 0)


def exchange_kernel(
    regions, devs, pairs,
    rates_ref, values_ref, row_ref, col_ref, deal_ref, index_ref, table_ref,
    signal_ref, source_ref, errors_ref, scale_ref,
    panels, panels16, following, out1, rates_in, block, work, out2, partials_in,
    mismatches, gradients, out3, signal_in,
    block_sem, send1, recv1, send_next, recv_next, send_pair, recv_pair,
    send2, recv2, send3, recv3,
):
    slots = regions * devs
    steps = slots * pairs
    rows = panels.shape[0]
    size = block.shape[0]
    group = size // LANES
    c = lax.axis_index("pair")
    q = lax.axis_index("region") * devs + lax.axis_index("dev")
    me = c * slots + q

    def at(slot, core):
        return {"region": slot // devs, "dev": slot % devs, "pair": core}

    load = pltpu.make_async_copy(values_ref.at[0], block, block_sem)
    load.start()

    barrier = pltpu.get_barrier_semaphore()

    def greet(i):
        other = lax.rem(me + 1 + i, steps)
        pl.semaphore_signal(
            barrier, inc=1, device_id=at(lax.rem(other, slots), other // slots), device_id_type=MESH
        )

    repeat(steps - 1, greet)

    def spread(i):
        lanes = pl.ds(i * LANES, LANES) if isinstance(i, int) else pl.ds(
            pl.multiple_of(i * LANES, LANES), LANES)
        panels[i // 8, pl.ds(i % 8, 1), :] = rates_ref[:, lanes].astype(jnp.float32)

    repeat(rows * 8, spread)
    panels16[...] = panels[...].astype(jnp.bfloat16)

    def pick(k):
        out1[k] = panels[col_ref[deal_ref[k]]].astype(jnp.bfloat16)

    repeat(slots, pick)
    rates_in[me] = panels[col_ref[deal_ref[q]]].astype(jnp.bfloat16)
    pl.semaphore_wait(barrier, steps - 1)

    def rates_copy(to, frm):
        return pltpu.make_async_remote_copy(
            src_ref=out1.at[to], dst_ref=rates_in.at[c * slots + frm],
            send_sem=send1.at[to], recv_sem=recv1.at[frm],
            device_id=at(to, c), device_id_type=MESH,
        )

    def send_rates(i):
        rates_copy(lax.rem(q + 1 + i, slots), q).start()

    repeat(slots - 1, send_rates)
    before = lax.rem(q * pairs + c + steps - 1, steps)
    next_copy = pltpu.make_async_remote_copy(
        src_ref=panels16, dst_ref=following, send_sem=send_next, recv_sem=recv_next,
        device_id=at(before // pairs, lax.rem(before, pairs)), device_id_type=MESH,
    )
    next_copy.start()

    for g in range(group):
        scale_ref[:, g * LANES:(g + 1) * LANES] = jnp.full(
            (1, LANES), table_ref[index_ref[0, g]], jnp.float32)
    load.wait()
    chunk = 64

    @pl.loop(0, size // chunk)
    def _(i):
        part = pl.ds(pl.multiple_of(i * chunk, chunk), chunk)
        block[part, :] = (block[part, :].astype(jnp.float32) * scale_ref[...]).astype(jnp.bfloat16)

    def wait_rates(i):
        rates_copy(lax.rem(q + 1 + i, slots), lax.rem(q + 1 + i, slots)).wait_recv()

    repeat(slots - 1, wait_rates)
    mine = pl.ds(c * slots, slots)
    pair_copy = pltpu.make_async_remote_copy(
        src_ref=rates_in.at[mine], dst_ref=rates_in.at[mine],
        send_sem=send_pair, recv_sem=recv_pair, device_id=at(q, 1 - c), device_id_type=MESH,
    )
    pair_copy.start()
    work[pl.ds(0, slots * 8), :] = rates_in[mine].astype(jnp.float32).reshape(slots * 8, LANES)
    source = jnp.concatenate(
        [work[pl.ds(j, slots, stride=8), :] for j in range(group)], axis=1).astype(jnp.bfloat16)
    partial_value = lax.dot_general(
        source, block[...], (((1,), (1,)), ((), ())), preferred_element_type=jnp.float32)
    for j in range(group):
        out2[pl.ds(j, slots, stride=8), :] = partial_value[:, j * LANES:(j + 1) * LANES]

    def tile(i):
        return pl.ds(pl.multiple_of(i * 8, 8), 8)

    def partial_copy(to, frm):
        return pltpu.make_async_remote_copy(
            src_ref=out2.at[tile(to)], dst_ref=partials_in.at[tile(frm)],
            send_sem=send2.at[to], recv_sem=recv2.at[frm],
            device_id=at(to, c), device_id_type=MESH,
        )

    def send_partial(i):
        partial_copy(lax.rem(q + 1 + i, slots), q).start()

    repeat(slots - 1, send_partial)
    partials_in[tile(q), :] = out2[tile(q), :]
    next_copy.wait_recv()

    def wait_partial(i):
        partial_copy(lax.rem(q + 1 + i, slots), lax.rem(q + 1 + i, slots)).wait_recv()

    repeat(slots - 1, wait_partial)
    valid = q * pairs + c < steps - 1

    def panel_step(r):
        def add(k, total):
            return total + jnp.where(
                row_ref[deal_ref[k]] == r, partials_in[pl.ds(pl.multiple_of(k * 8, 8), 8), :], 0.0)

        total = jnp.zeros((8, LANES), jnp.float32)
        if slots <= 32:
            for k in range(slots):
                total = add(k, total)
        else:
            total = lax.fori_loop(0, slots, add, total)
        predicted = jnp.tanh(total)
        target = following[r].astype(jnp.float32)
        mismatch = jnp.where(valid, predicted - target, 0.0)
        mismatches[tile(r), :] = mismatch
        gradients[r] = mismatch * (1.0 - predicted * predicted) * (1.0 / math.sqrt(steps))

    repeat(rows, panel_step)

    def pick_signal(k):
        out3[k] = gradients[row_ref[deal_ref[k]]].astype(jnp.bfloat16)

    repeat(slots, pick_signal)

    def signal_copy(to, frm):
        to_slot, to_core = lax.rem(to, slots), to // slots
        return pltpu.make_async_remote_copy(
            src_ref=out3.at[to_slot], dst_ref=signal_in.at[frm],
            send_sem=send3.at[to], recv_sem=recv3.at[frm],
            device_id=at(to_slot, to_core), device_id_type=MESH,
        )

    def send_signal(i):
        signal_copy(lax.rem(me + 1 + i, steps), me).start()

    repeat(steps - 1, send_signal)
    signal_in[me] = gradients[row_ref[deal_ref[q]]].astype(jnp.bfloat16)

    def gather_errors(i):
        lanes = pl.ds(i * LANES, LANES) if isinstance(i, int) else pl.ds(
            pl.multiple_of(i * LANES, LANES), LANES)
        errors_ref[:, lanes] = mismatches[pl.ds(i, 1), :].astype(jnp.bfloat16)

    repeat(rows * 8, gather_errors)
    pair_copy.wait_recv()
    work[...] = rates_in[...].astype(jnp.float32).reshape(steps * 8, LANES)
    for j in range(group):
        source_ref[:, j * LANES:(j + 1) * LANES] = work[pl.ds(j, steps, stride=8), :].astype(
            jnp.bfloat16)

    def drain(i):
        to = lax.rem(q + 1 + i, slots)
        rates_copy(to, q).wait_send()
        partial_copy(to, q).wait_send()

    repeat(slots - 1, drain)
    next_copy.wait_send()
    pair_copy.wait_send()

    def wait_signal(i):
        signal_copy(lax.rem(me + 1 + i, steps), lax.rem(me + 1 + i, steps)).wait_recv()

    repeat(steps - 1, wait_signal)
    work[...] = signal_in[...].astype(jnp.float32).reshape(steps * 8, LANES)
    half = group // pairs
    for j in range(half):
        signal_ref[:, j * LANES:(j + 1) * LANES] = work[
            pl.ds(c * half + j, steps, stride=8), :].astype(jnp.bfloat16)

    def drain_signal(i):
        signal_copy(lax.rem(me + 1 + i, steps), me).wait_send()

    repeat(steps - 1, drain_signal)


def gradient_kernel(signal_ref, source_ref, scale_ref, errors_ref, grads_ref, errors_out):
    term = lax.dot_general(
        signal_ref[...], source_ref[...], (((0,), (0,)), ((), ())),
        preferred_element_type=jnp.float32)
    grads_ref[0] = (term * scale_ref[...]).astype(jnp.bfloat16)
    errors_out[...] = errors_ref[...]


def shards(sizes, observed_rates, block_values, block_row, block_col, deal_list, scale_index,
           scale_table):
    regions, devs, pairs = sizes
    slots = regions * devs
    steps = slots * pairs
    neurons = observed_rates.shape[1]
    size = block_values.shape[1]
    rows = neurons // size
    bf16, f32 = jnp.bfloat16, jnp.float32
    vmem = pl.BlockSpec(memory_space=pltpu.VMEM)
    smem = pl.BlockSpec(memory_space=pltpu.SMEM)
    dma = pltpu.SemaphoreType.DMA
    signal, source, errors, scale = pl.pallas_call(
        functools.partial(exchange_kernel, regions, devs, pairs),
        out_shape=(
            jax.ShapeDtypeStruct((steps, size // pairs), bf16),
            jax.ShapeDtypeStruct((steps, size), bf16),
            jax.ShapeDtypeStruct((1, neurons), bf16),
            jax.ShapeDtypeStruct((1, size), f32),
        ),
        in_specs=[vmem, pl.BlockSpec(memory_space=pl.ANY)] + [smem] * 5,
        out_specs=(vmem,) * 4,
        scratch_shapes=[
            pltpu.VMEM((rows, 8, LANES), f32),
            pltpu.VMEM((rows, 8, LANES), bf16),
            pltpu.VMEM((rows, 8, LANES), bf16),
            pltpu.VMEM((slots, 8, LANES), bf16),
            pltpu.VMEM((steps, 8, LANES), bf16),
            pltpu.VMEM((size, size), bf16),
            pltpu.VMEM((steps * 8, LANES), f32),
            pltpu.VMEM((slots * 8, LANES), f32),
            pltpu.VMEM((slots * 8, LANES), f32),
            pltpu.VMEM((rows * 8, LANES), f32),
            pltpu.VMEM((rows, 8, LANES), f32),
            pltpu.VMEM((slots, 8, LANES), bf16),
            pltpu.VMEM((steps, 8, LANES), bf16),
            dma, dma((slots,)), dma((slots,)), dma, dma, dma, dma,
            dma((slots,)), dma((slots,)), dma((steps,)), dma((steps,)),
        ],
        compiler_params=pltpu.CompilerParams(
            collective_id=0, has_side_effects=True, vmem_limit_bytes=32 * 1024 * 1024),
        name="exchange",
    )(observed_rates, block_values, block_row, block_col, deal_list, scale_index, scale_table)
    grads, errors = pl.pallas_call(
        gradient_kernel,
        out_shape=(
            jax.ShapeDtypeStruct((1, size // pairs, size), bf16),
            jax.ShapeDtypeStruct((1, neurons), bf16),
        ),
        in_specs=[vmem] * 4,
        out_specs=(vmem, vmem),
        compiler_params=pltpu.CompilerParams(vmem_limit_bytes=32 * 1024 * 1024),
        name="gradient",
    )(signal, source, scale, errors)
    return (errors, grads)


def solution(mesh):
    sizes = (mesh.shape["region"], mesh.shape["dev"], mesh.shape["pair"])
    return jax.shard_map(
        functools.partial(shards, sizes),
        mesh=mesh,
        in_specs=(
            P(("parts", "region", "dev", "pair"), None),
            P(("parts", "region", "dev"), None, None),
            P("parts"),
            P("parts"),
            P("parts"),
            P(("parts", "region", "dev"), None),
            P("parts"),
        ),
        out_specs=(
            P(("parts", "region", "dev", "pair"), None),
            P(("parts", "region", "dev"), "pair", None),
        ),
        check_vma=False,
    )
```

```python
import functools
import math

import jax
import jax.numpy as jnp
from jax import lax
from jax.experimental import pallas as pl
from jax.experimental.pallas import tpu as pltpu
from jax.sharding import PartitionSpec as P

LANES = 128
MESH = pl.DeviceIdType.MESH


def repeat(count, body):
    if count <= 32:
        for i in range(count):
            body(i)
    else:
        lax.fori_loop(0, count, lambda i, carry: (body(i), carry)[1], 0)


def exchange_kernel(
    regions, devs, pairs,
    rates_hbm, values_hbm, row_hbm, col_hbm, deal_hbm, index_hbm, table_hbm,
    signal_ref, source_ref, errors_ref, scale_ref,
    panels, panels16, following, out1, rates_in, block, work, out2, partials_in,
    mismatches, gradients, out3, signal_in,
    rates_ref, row_ref, col_ref, deal_ref, index_ref, table_ref, small_sem,
    block_sem, send1, recv1, send_next, recv_next, send_pair, recv_pair,
    send2, recv2, send3, recv3,
):
    slots = regions * devs
    steps = slots * pairs
    rows = panels.shape[0]
    size = block.shape[0]
    group = size // LANES
    c = lax.axis_index("pair")
    q = lax.axis_index("region") * devs + lax.axis_index("dev")
    me = c * slots + q

    def at(slot, core):
        return {"region": slot // devs, "dev": slot % devs, "pair": core}

    smalls = [
        pltpu.make_async_copy(source, held, small_sem.at[i])
        for i, (source, held) in enumerate((
            (rates_hbm, rates_ref), (col_hbm, col_ref), (deal_hbm, deal_ref),
            (row_hbm, row_ref), (index_hbm, index_ref), (table_hbm, table_ref)))
    ]
    for copy in smalls:
        copy.start()
    load = pltpu.make_async_copy(values_hbm.at[0], block, block_sem)
    load.start()

    barrier = pltpu.get_barrier_semaphore()

    def greet(i):
        other = lax.rem(me + 1 + i, steps)
        pl.semaphore_signal(
            barrier, inc=1, device_id=at(lax.rem(other, slots), other // slots), device_id_type=MESH
        )

    repeat(steps - 1, greet)

    for copy in smalls:
        copy.wait()

    def spread(i):
        lanes = pl.ds(i * LANES, LANES) if isinstance(i, int) else pl.ds(
            pl.multiple_of(i * LANES, LANES), LANES)
        panels[i // 8, pl.ds(i % 8, 1), :] = rates_ref[:, lanes].astype(jnp.float32)

    repeat(rows * 8, spread)
    panels16[...] = panels[...].astype(jnp.bfloat16)

    def pick(k):
        out1[k] = panels[col_ref[deal_ref[k]]].astype(jnp.bfloat16)

    repeat(slots, pick)
    rates_in[me] = panels[col_ref[deal_ref[q]]].astype(jnp.bfloat16)
    pl.semaphore_wait(barrier, steps - 1)

    def rates_copy(to, frm):
        return pltpu.make_async_remote_copy(
            src_ref=out1.at[to], dst_ref=rates_in.at[c * slots + frm],
            send_sem=send1.at[to], recv_sem=recv1.at[frm],
            device_id=at(to, c), device_id_type=MESH,
        )

    def send_rates(i):
        rates_copy(lax.rem(q + 1 + i, slots), q).start()

    repeat(slots - 1, send_rates)
    before = lax.rem(q * pairs + c + steps - 1, steps)
    next_copy = pltpu.make_async_remote_copy(
        src_ref=panels16, dst_ref=following, send_sem=send_next, recv_sem=recv_next,
        device_id=at(before // pairs, lax.rem(before, pairs)), device_id_type=MESH,
    )
    next_copy.start()

    for g in range(group):
        scale_ref[:, g * LANES:(g + 1) * LANES] = jnp.full(
            (1, LANES), table_ref[index_ref[0, g]], jnp.float32)
    load.wait()
    chunk = 64

    @pl.loop(0, size // chunk)
    def _(i):
        part = pl.ds(pl.multiple_of(i * chunk, chunk), chunk)
        block[part, :] = (block[part, :].astype(jnp.float32) * scale_ref[...]).astype(jnp.bfloat16)

    def wait_rates(i):
        rates_copy(lax.rem(q + 1 + i, slots), lax.rem(q + 1 + i, slots)).wait_recv()

    repeat(slots - 1, wait_rates)
    mine = pl.ds(c * slots, slots)
    pair_copy = pltpu.make_async_remote_copy(
        src_ref=rates_in.at[mine], dst_ref=rates_in.at[mine],
        send_sem=send_pair, recv_sem=recv_pair, device_id=at(q, 1 - c), device_id_type=MESH,
    )
    pair_copy.start()
    work[pl.ds(0, slots * 8), :] = rates_in[mine].astype(jnp.float32).reshape(slots * 8, LANES)
    source = jnp.concatenate(
        [work[pl.ds(j, slots, stride=8), :] for j in range(group)], axis=1).astype(jnp.bfloat16)
    partial_value = lax.dot_general(
        source, block[...], (((1,), (1,)), ((), ())), preferred_element_type=jnp.float32)
    for j in range(group):
        out2[pl.ds(j, slots, stride=8), :] = partial_value[:, j * LANES:(j + 1) * LANES]

    def tile(i):
        return pl.ds(pl.multiple_of(i * 8, 8), 8)

    def partial_copy(to, frm):
        return pltpu.make_async_remote_copy(
            src_ref=out2.at[tile(to)], dst_ref=partials_in.at[tile(frm)],
            send_sem=send2.at[to], recv_sem=recv2.at[frm],
            device_id=at(to, c), device_id_type=MESH,
        )

    def send_partial(i):
        partial_copy(lax.rem(q + 1 + i, slots), q).start()

    repeat(slots - 1, send_partial)
    partials_in[tile(q), :] = out2[tile(q), :]
    next_copy.wait_recv()

    def wait_partial(i):
        partial_copy(lax.rem(q + 1 + i, slots), lax.rem(q + 1 + i, slots)).wait_recv()

    repeat(slots - 1, wait_partial)
    valid = q * pairs + c < steps - 1

    def panel_step(r):
        def add(k, total):
            return total + jnp.where(
                row_ref[deal_ref[k]] == r, partials_in[pl.ds(pl.multiple_of(k * 8, 8), 8), :], 0.0)

        total = jnp.zeros((8, LANES), jnp.float32)
        if slots <= 32:
            for k in range(slots):
                total = add(k, total)
        else:
            total = lax.fori_loop(0, slots, add, total)
        predicted = jnp.tanh(total)
        target = following[r].astype(jnp.float32)
        mismatch = jnp.where(valid, predicted - target, 0.0)
        mismatches[tile(r), :] = mismatch
        gradients[r] = mismatch * (1.0 - predicted * predicted) * (1.0 / math.sqrt(steps))

    repeat(rows, panel_step)

    def pick_signal(k):
        out3[k] = gradients[row_ref[deal_ref[k]]].astype(jnp.bfloat16)

    repeat(slots, pick_signal)

    def signal_copy(to, frm):
        to_slot, to_core = lax.rem(to, slots), to // slots
        return pltpu.make_async_remote_copy(
            src_ref=out3.at[to_slot], dst_ref=signal_in.at[frm],
            send_sem=send3.at[to], recv_sem=recv3.at[frm],
            device_id=at(to_slot, to_core), device_id_type=MESH,
        )

    def send_signal(i):
        signal_copy(lax.rem(me + 1 + i, steps), me).start()

    repeat(steps - 1, send_signal)
    signal_in[me] = gradients[row_ref[deal_ref[q]]].astype(jnp.bfloat16)

    def gather_errors(i):
        lanes = pl.ds(i * LANES, LANES) if isinstance(i, int) else pl.ds(
            pl.multiple_of(i * LANES, LANES), LANES)
        errors_ref[:, lanes] = mismatches[pl.ds(i, 1), :].astype(jnp.bfloat16)

    repeat(rows * 8, gather_errors)
    pair_copy.wait_recv()
    work[...] = rates_in[...].astype(jnp.float32).reshape(steps * 8, LANES)
    for j in range(group):
        source_ref[:, j * LANES:(j + 1) * LANES] = work[pl.ds(j, steps, stride=8), :].astype(
            jnp.bfloat16)

    def drain(i):
        to = lax.rem(q + 1 + i, slots)
        rates_copy(to, q).wait_send()
        partial_copy(to, q).wait_send()

    repeat(slots - 1, drain)
    next_copy.wait_send()
    pair_copy.wait_send()

    def wait_signal(i):
        signal_copy(lax.rem(me + 1 + i, steps), lax.rem(me + 1 + i, steps)).wait_recv()

    repeat(steps - 1, wait_signal)
    work[...] = signal_in[...].astype(jnp.float32).reshape(steps * 8, LANES)
    half = group // pairs
    for j in range(half):
        signal_ref[:, j * LANES:(j + 1) * LANES] = work[
            pl.ds(c * half + j, steps, stride=8), :].astype(jnp.bfloat16)

    def drain_signal(i):
        signal_copy(lax.rem(me + 1 + i, steps), me).wait_send()

    repeat(steps - 1, drain_signal)


def gradient_kernel(signal_ref, source_ref, scale_ref, errors_ref, grads_ref, errors_out):
    term = lax.dot_general(
        signal_ref[...], source_ref[...], (((0,), (0,)), ((), ())),
        preferred_element_type=jnp.float32)
    grads_ref[0] = (term * scale_ref[...]).astype(jnp.bfloat16)
    errors_out[...] = errors_ref[...]


def shards(sizes, observed_rates, block_values, block_row, block_col, deal_list, scale_index,
           scale_table):
    regions, devs, pairs = sizes
    slots = regions * devs
    steps = slots * pairs
    neurons = observed_rates.shape[1]
    size = block_values.shape[1]
    rows = neurons // size
    bf16, f32 = jnp.bfloat16, jnp.float32
    vmem = pl.BlockSpec(memory_space=pltpu.VMEM)
    dma = pltpu.SemaphoreType.DMA
    signal, source, errors, scale = pl.pallas_call(
        functools.partial(exchange_kernel, regions, devs, pairs),
        out_shape=(
            jax.ShapeDtypeStruct((steps, size // pairs), bf16),
            jax.ShapeDtypeStruct((steps, size), bf16),
            jax.ShapeDtypeStruct((1, neurons), bf16),
            jax.ShapeDtypeStruct((1, size), f32),
        ),
        in_specs=[pl.BlockSpec(memory_space=pltpu.HBM)] * 7,
        out_specs=(vmem,) * 4,
        scratch_shapes=[
            pltpu.VMEM((rows, 8, LANES), f32),
            pltpu.VMEM((rows, 8, LANES), bf16),
            pltpu.VMEM((rows, 8, LANES), bf16),
            pltpu.VMEM((slots, 8, LANES), bf16),
            pltpu.VMEM((steps, 8, LANES), bf16),
            pltpu.VMEM((size, size), bf16),
            pltpu.VMEM((steps * 8, LANES), f32),
            pltpu.VMEM((slots * 8, LANES), f32),
            pltpu.VMEM((slots * 8, LANES), f32),
            pltpu.VMEM((rows * 8, LANES), f32),
            pltpu.VMEM((rows, 8, LANES), f32),
            pltpu.VMEM((slots, 8, LANES), bf16),
            pltpu.VMEM((steps, 8, LANES), bf16),
            pltpu.VMEM((1, neurons), bf16),
            pltpu.SMEM(block_row.shape, jnp.int32),
            pltpu.SMEM(block_col.shape, jnp.int32),
            pltpu.SMEM(deal_list.shape, jnp.int32),
            pltpu.SMEM(scale_index.shape, jnp.int32),
            pltpu.SMEM(scale_table.shape, f32),
            dma((6,)),
            dma, dma((slots,)), dma((slots,)), dma, dma, dma, dma,
            dma((slots,)), dma((slots,)), dma((steps,)), dma((steps,)),
        ],
        compiler_params=pltpu.CompilerParams(
            collective_id=0, has_side_effects=True, vmem_limit_bytes=32 * 1024 * 1024),
        name="exchange",
    )(*(pltpu.with_memory_space_constraint(operand, pltpu.HBM) for operand in (
        observed_rates, block_values, block_row, block_col, deal_list, scale_index, scale_table)))
    grads, errors = pl.pallas_call(
        gradient_kernel,
        out_shape=(
            jax.ShapeDtypeStruct((1, size // pairs, size), bf16),
            jax.ShapeDtypeStruct((1, neurons), bf16),
        ),
        in_specs=[vmem] * 4,
        out_specs=(vmem, vmem),
        compiler_params=pltpu.CompilerParams(vmem_limit_bytes=32 * 1024 * 1024),
        name="gradient",
    )(signal, source, scale, errors)
    return (errors, grads)


def solution(mesh):
    sizes = (mesh.shape["region"], mesh.shape["dev"], mesh.shape["pair"])
    return jax.shard_map(
        functools.partial(shards, sizes),
        mesh=mesh,
        in_specs=(
            P(("parts", "region", "dev", "pair"), None),
            P(("parts", "region", "dev"), None, None),
            P("parts"),
            P("parts"),
            P("parts"),
            P(("parts", "region", "dev"), None),
            P("parts"),
        ),
        out_specs=(
            P(("parts", "region", "dev", "pair"), None),
            P(("parts", "region", "dev"), "pair", None),
        ),
        check_vma=False,
    )
```

```python
import functools
import math

import jax
import jax.numpy as jnp
from jax import lax
from jax.experimental import pallas as pl
from jax.experimental.pallas import tpu as pltpu
from jax.sharding import PartitionSpec as P

LANES = 128
MESH = pl.DeviceIdType.MESH


def repeat(count, body):
    if count <= 32:
        for i in range(count):
            body(i)
    else:
        lax.fori_loop(0, count, lambda i, carry: (body(i), carry)[1], 0)


def exchange_kernel(
    regions, devs, pairs,
    rates_hbm, values_hbm, row_hbm, col_hbm, deal_hbm, index_hbm, table_hbm,
    signal_ref, source_ref, errors_ref, scale_ref,
    panels, panels16, following, out1, rates_in, block, work, halves, halves_in, out2, partials_in,
    mismatches,
    rates_ref, row_ref, col_ref, deal_ref, index_ref, table_ref, small_sem,
    block_sem, send1, recv1, send_next, recv_next, send2, recv2, send3, recv3,
):
    slots = regions * devs
    steps = slots * pairs
    rows = panels.shape[0]
    half = block.shape[0]
    group = block.shape[1] // LANES
    part = half // LANES
    c = lax.axis_index("pair")
    q = lax.axis_index("region") * devs + lax.axis_index("dev")
    me = q * pairs + c

    def at(slot, core):
        return {"region": slot // devs, "dev": slot % devs, "pair": core}

    def at_step(step):
        return at(step // pairs, lax.rem(step, pairs))

    def other_step(i):
        return lax.rem(me + 1 + i, steps)

    def other_slot(i):
        return lax.rem(q + 1 + i, slots)

    def tile(i):
        return pl.ds(pl.multiple_of(i * 8, 8), 8)

    def lanes_of(i):
        return pl.ds(i * LANES, LANES) if isinstance(i, int) else pl.ds(
            pl.multiple_of(i * LANES, LANES), LANES)

    smalls = [
        pltpu.make_async_copy(source, held, small_sem.at[i])
        for i, (source, held) in enumerate((
            (rates_hbm, rates_ref), (col_hbm, col_ref), (deal_hbm, deal_ref),
            (row_hbm, row_ref), (index_hbm, index_ref), (table_hbm, table_ref)))
    ]
    for copy in smalls:
        copy.start()
    load = pltpu.make_async_copy(
        values_hbm.at[0, pl.ds(pl.multiple_of(c * half, half), half)], block, block_sem)
    load.start()

    barrier = pltpu.get_barrier_semaphore()

    def greet(i):
        pl.semaphore_signal(
            barrier, inc=1, device_id=at_step(other_step(i)), device_id_type=MESH)

    repeat(steps - 1, greet)
    for copy in smalls:
        copy.wait()

    def spread(i):
        panels[i // 8, pl.ds(i % 8, 1), :] = rates_ref[:, lanes_of(i)].astype(jnp.float32)

    repeat(rows * 8, spread)
    panels16[...] = panels[...].astype(jnp.bfloat16)

    def pick(k):
        out1[k, 0] = panels[col_ref[deal_ref[k]]].astype(jnp.bfloat16)
        out1[k, 1] = panels[row_ref[deal_ref[k]]].astype(jnp.bfloat16)

    repeat(slots, pick)
    my_row = row_ref[deal_ref[q]]
    rates_in[me, 0] = panels[col_ref[deal_ref[q]]].astype(jnp.bfloat16)
    rates_in[me, 1] = panels[my_row].astype(jnp.bfloat16)
    rates_in[steps] = jnp.zeros(rates_in.shape[1:], jnp.bfloat16)
    pl.semaphore_wait(barrier, steps - 1)

    def rates_copy(to, frm):
        return pltpu.make_async_remote_copy(
            src_ref=out1.at[to // pairs], dst_ref=rates_in.at[frm],
            send_sem=send1.at[to], recv_sem=recv1.at[frm],
            device_id=at_step(to), device_id_type=MESH,
        )

    repeat(steps - 1, lambda i: rates_copy(other_step(i), me).start())
    next_copy = pltpu.make_async_remote_copy(
        src_ref=panels16, dst_ref=following, send_sem=send_next, recv_sem=recv_next,
        device_id=at_step(lax.rem(me + steps - 1, steps)), device_id_type=MESH,
    )
    next_copy.start()

    for g in range(group):
        scale_ref[:, g * LANES:(g + 1) * LANES] = jnp.full(
            (1, LANES), table_ref[index_ref[0, g]], jnp.float32)

    def same_row(k, found):
        return jnp.maximum(found, jnp.where((row_ref[deal_ref[k]] == my_row) & (k != q), k, 0))

    partner = jnp.int32(0)
    if slots <= 32:
        for k in range(slots):
            partner = same_row(k, partner)
    else:
        partner = lax.fori_loop(0, slots, same_row, partner)
    load.wait()
    chunk = 64

    @pl.loop(0, half // chunk)
    def _(i):
        piece = pl.ds(pl.multiple_of(i * chunk, chunk), chunk)
        block[piece, :] = (block[piece, :].astype(jnp.float32) * scale_ref[...]).astype(
            jnp.bfloat16)

    repeat(steps - 1, lambda i: rates_copy(other_step(i), other_step(i)).wait_recv())
    work[...] = rates_in[pl.ds(0, steps), 0].astype(jnp.float32).reshape(steps * 8, LANES)
    for j in range(group):
        source_ref[:, j * LANES:(j + 1) * LANES] = work[pl.ds(j, steps, stride=8), :].astype(
            jnp.bfloat16)
    partial_value = lax.dot_general(
        source_ref[...], block[...], (((1,), (1,)), ((), ())), preferred_element_type=jnp.float32)
    halves[...] = partial_value.astype(jnp.bfloat16)
    halves_in[q] = halves[...]

    def half_copy(to, frm):
        return pltpu.make_async_remote_copy(
            src_ref=halves, dst_ref=halves_in.at[frm],
            send_sem=send2.at[to], recv_sem=recv2.at[frm],
            device_id=at(to, c), device_id_type=MESH,
        )

    repeat(slots - 1, lambda i: half_copy(other_slot(i), q).start())
    for j in range(8):
        k = j % part
        out2[pl.ds(j, steps, stride=8), :] = partial_value[:, k * LANES:(k + 1) * LANES]

    def partial_copy(to, frm):
        return pltpu.make_async_remote_copy(
            src_ref=out2.at[tile(to)], dst_ref=partials_in.at[tile(frm)],
            send_sem=send3.at[to], recv_sem=recv3.at[frm],
            device_id=at_step(to), device_id_type=MESH,
        )

    repeat(steps - 1, lambda i: partial_copy(other_step(i), me).start())
    partials_in[tile(me), :] = out2[tile(me), :]
    work[...] = rates_in[pl.ds(1, steps), 1].astype(jnp.float32).reshape(steps * 8, LANES)
    target = jnp.concatenate(
        [work[pl.ds(c * part + j, steps, stride=8), :] for j in range(part)], axis=1)
    row = lax.broadcasted_iota(jnp.int32, (steps, half), 0)
    repeat(steps - 1, lambda i: rates_copy(other_step(i), me).wait_send())
    next_copy.wait()

    repeat(slots - 1, lambda i: half_copy(other_slot(i), other_slot(i)).wait_recv())
    scale = 1.0 / math.sqrt(steps)
    predicted = jnp.tanh(partial_value + halves_in[partner].astype(jnp.float32))
    mismatch = jnp.where(row < steps - 1, predicted - target, 0.0)
    signal_ref[...] = (mismatch * (1.0 - predicted * predicted) * scale).astype(jnp.bfloat16)

    repeat(steps - 1, lambda i: partial_copy(other_step(i), other_step(i)).wait_recv())

    def panel_step(r):
        def add(k, total):
            value = jnp.concatenate(
                [partials_in[tile(k * pairs + core), :][:part] for core in range(pairs)], axis=0)
            return total + jnp.where(row_ref[deal_ref[k]] == r, value, 0.0)

        total = jnp.zeros((8, LANES), jnp.float32)
        if slots <= 32:
            for k in range(slots):
                total = add(k, total)
        else:
            total = lax.fori_loop(0, slots, add, total)
        mismatches[tile(r), :] = jnp.where(
            me < steps - 1, jnp.tanh(total) - following[r].astype(jnp.float32), 0.0)

    repeat(rows, panel_step)

    def gather_errors(i):
        errors_ref[:, lanes_of(i)] = mismatches[pl.ds(i, 1), :].astype(jnp.bfloat16)

    repeat(rows * 8, gather_errors)
    repeat(slots - 1, lambda i: half_copy(other_slot(i), q).wait_send())
    repeat(steps - 1, lambda i: partial_copy(other_step(i), me).wait_send())


def gradient_kernel(signal_ref, source_ref, scale_ref, errors_ref, grads_ref, errors_out):
    term = lax.dot_general(
        signal_ref[...], source_ref[...], (((0,), (0,)), ((), ())),
        preferred_element_type=jnp.float32)
    grads_ref[0] = (term * scale_ref[...]).astype(jnp.bfloat16)
    errors_out[...] = errors_ref[...]


def shards(sizes, observed_rates, block_values, block_row, block_col, deal_list, scale_index,
           scale_table):
    regions, devs, pairs = sizes
    slots = regions * devs
    steps = slots * pairs
    neurons = observed_rates.shape[1]
    size = block_values.shape[1]
    rows = neurons // size
    bf16, f32 = jnp.bfloat16, jnp.float32
    vmem = pl.BlockSpec(memory_space=pltpu.VMEM)
    dma = pltpu.SemaphoreType.DMA
    signal, source, errors, scale = pl.pallas_call(
        functools.partial(exchange_kernel, regions, devs, pairs),
        out_shape=(
            jax.ShapeDtypeStruct((steps, size // pairs), bf16),
            jax.ShapeDtypeStruct((steps, size), bf16),
            jax.ShapeDtypeStruct((1, neurons), bf16),
            jax.ShapeDtypeStruct((1, size), f32),
        ),
        in_specs=[pl.BlockSpec(memory_space=pltpu.HBM)] * 7,
        out_specs=(vmem,) * 4,
        scratch_shapes=[
            pltpu.VMEM((rows, 8, LANES), f32),
            pltpu.VMEM((rows, 8, LANES), bf16),
            pltpu.VMEM((rows, 8, LANES), bf16),
            pltpu.VMEM((slots, 2, 8, LANES), bf16),
            pltpu.VMEM((steps + 1, 2, 8, LANES), bf16),
            pltpu.VMEM((size // pairs, size), bf16),
            pltpu.VMEM((steps * 8, LANES), f32),
            pltpu.VMEM((steps, size // pairs), bf16),
            pltpu.VMEM((slots, steps, size // pairs), bf16),
            pltpu.VMEM((steps * 8, LANES), f32),
            pltpu.VMEM((steps * 8, LANES), f32),
            pltpu.VMEM((rows * 8, LANES), f32),
            pltpu.VMEM((1, neurons), bf16),
            pltpu.SMEM(block_row.shape, jnp.int32),
            pltpu.SMEM(block_col.shape, jnp.int32),
            pltpu.SMEM(deal_list.shape, jnp.int32),
            pltpu.SMEM(scale_index.shape, jnp.int32),
            pltpu.SMEM(scale_table.shape, f32),
            dma((6,)),
            dma, dma((steps,)), dma((steps,)), dma, dma,
            dma((slots,)), dma((slots,)), dma((steps,)), dma((steps,)),
        ],
        compiler_params=pltpu.CompilerParams(
            collective_id=0, has_side_effects=True, vmem_limit_bytes=48 * 1024 * 1024),
        name="exchange",
    )(*(pltpu.with_memory_space_constraint(operand, pltpu.HBM) for operand in (
        observed_rates, block_values, block_row, block_col, deal_list, scale_index, scale_table)))
    grads, errors = pl.pallas_call(
        gradient_kernel,
        out_shape=(
            jax.ShapeDtypeStruct((1, size // pairs, size), bf16),
            jax.ShapeDtypeStruct((1, neurons), bf16),
        ),
        in_specs=[vmem] * 4,
        out_specs=(vmem, vmem),
        compiler_params=pltpu.CompilerParams(vmem_limit_bytes=32 * 1024 * 1024),
        name="gradient",
    )(signal, source, scale, errors)
    return (errors, grads)


def solution(mesh):
    sizes = (mesh.shape["region"], mesh.shape["dev"], mesh.shape["pair"])
    return jax.shard_map(
        functools.partial(shards, sizes),
        mesh=mesh,
        in_specs=(
            P(("parts", "region", "dev", "pair"), None),
            P(("parts", "region", "dev"), None, None),
            P("parts"),
            P("parts"),
            P("parts"),
            P(("parts", "region", "dev"), None),
            P("parts"),
        ),
        out_specs=(
            P(("parts", "region", "dev", "pair"), None),
            P(("parts", "region", "dev"), "pair", None),
        ),
        check_vma=False,
    )
```

```python
import functools
import math

import jax
import jax.numpy as jnp
from jax import lax
from jax.experimental import pallas as pl
from jax.experimental.pallas import tpu as pltpu
from jax.sharding import PartitionSpec as P

LANES = 128
MESH = pl.DeviceIdType.MESH


def repeat(count, body):
    if count <= 32:
        for i in range(count):
            body(i)
    else:
        lax.fori_loop(0, count, lambda i, carry: (body(i), carry)[1], 0)


def exchange_kernel(
    regions, devs, pairs,
    rates_hbm, values_hbm, row_hbm, col_hbm, deal_hbm, index_hbm, table_hbm,
    signal_ref, source_ref, errors_ref, scale_ref,
    panels, panels16, following, out1, rates_in, block, work, halves, halves_in, sums,
    target_row,
    rates_ref, row_ref, col_ref, deal_ref, index_ref, table_ref, small_sem,
    block_sem, send1, recv1, send_next, recv_next, send2, recv2, send3, recv3,
):
    slots = regions * devs
    steps = slots * pairs
    rows = panels.shape[0]
    half = block.shape[0]
    group = block.shape[1] // LANES
    part = half // LANES
    c = lax.axis_index("pair")
    q = lax.axis_index("region") * devs + lax.axis_index("dev")
    me = q * pairs + c

    def at(slot, core):
        return {"region": slot // devs, "dev": slot % devs, "pair": core}

    def at_step(step):
        return at(step // pairs, lax.rem(step, pairs))

    def other_step(i):
        return lax.rem(me + 1 + i, steps)

    def other_slot(i):
        return lax.rem(q + 1 + i, slots)

    def lanes_of(i):
        return pl.ds(i * LANES, LANES) if isinstance(i, int) else pl.ds(
            pl.multiple_of(i * LANES, LANES), LANES)

    smalls = [
        pltpu.make_async_copy(source, held, small_sem.at[i])
        for i, (source, held) in enumerate((
            (rates_hbm, rates_ref), (col_hbm, col_ref), (deal_hbm, deal_ref),
            (row_hbm, row_ref), (index_hbm, index_ref), (table_hbm, table_ref)))
    ]
    for copy in smalls:
        copy.start()
    load = pltpu.make_async_copy(
        values_hbm.at[0, pl.ds(pl.multiple_of(c * half, half), half)], block, block_sem)
    load.start()

    barrier = pltpu.get_barrier_semaphore()

    def greet(i):
        pl.semaphore_signal(
            barrier, inc=1, device_id=at_step(other_step(i)), device_id_type=MESH)

    repeat(steps - 1, greet)
    for copy in smalls:
        copy.wait()

    def spread(i):
        panels[i // 8, pl.ds(i % 8, 1), :] = rates_ref[:, lanes_of(i)].astype(jnp.float32)

    repeat(rows * 8, spread)
    panels16[...] = panels[...].astype(jnp.bfloat16)

    def pick(k):
        out1[k, 0] = panels[col_ref[deal_ref[k]]].astype(jnp.bfloat16)
        out1[k, 1] = panels[row_ref[deal_ref[k]]].astype(jnp.bfloat16)

    repeat(slots, pick)
    my_row = row_ref[deal_ref[q]]
    rates_in[me, 0] = panels[col_ref[deal_ref[q]]].astype(jnp.bfloat16)
    rates_in[me, 1] = panels[my_row].astype(jnp.bfloat16)
    rates_in[steps] = jnp.zeros(rates_in.shape[1:], jnp.bfloat16)
    pl.semaphore_wait(barrier, steps - 1)

    def rates_copy(to, frm):
        return pltpu.make_async_remote_copy(
            src_ref=out1.at[to // pairs], dst_ref=rates_in.at[frm],
            send_sem=send1.at[to], recv_sem=recv1.at[frm],
            device_id=at_step(to), device_id_type=MESH,
        )

    repeat(steps - 1, lambda i: rates_copy(other_step(i), me).start())
    next_copy = pltpu.make_async_remote_copy(
        src_ref=panels16, dst_ref=following, send_sem=send_next, recv_sem=recv_next,
        device_id=at_step(lax.rem(me + steps - 1, steps)), device_id_type=MESH,
    )
    next_copy.start()

    for g in range(group):
        scale_ref[:, g * LANES:(g + 1) * LANES] = jnp.full(
            (1, LANES), table_ref[index_ref[0, g]], jnp.float32)

    def same_row(k, found):
        return jnp.maximum(found, jnp.where((row_ref[deal_ref[k]] == my_row) & (k != q), k, 0))

    partner = jnp.int32(0)
    if slots <= 32:
        for k in range(slots):
            partner = same_row(k, partner)
    else:
        partner = lax.fori_loop(0, slots, same_row, partner)
    load.wait()
    chunk = 64

    @pl.loop(0, half // chunk)
    def _(i):
        piece = pl.ds(pl.multiple_of(i * chunk, chunk), chunk)
        block[piece, :] = (block[piece, :].astype(jnp.float32) * scale_ref[...]).astype(
            jnp.bfloat16)

    repeat(steps - 1, lambda i: rates_copy(other_step(i), other_step(i)).wait_recv())
    work[...] = rates_in[pl.ds(0, steps), 0].astype(jnp.float32).reshape(steps * 8, LANES)
    for j in range(group):
        source_ref[:, j * LANES:(j + 1) * LANES] = work[pl.ds(j, steps, stride=8), :].astype(
            jnp.bfloat16)
    partial_value = lax.dot_general(
        source_ref[...], block[...], (((1,), (1,)), ((), ())), preferred_element_type=jnp.float32)
    halves[...] = partial_value.astype(jnp.bfloat16)
    halves_in[q] = halves[...]

    def half_copy(to, frm):
        return pltpu.make_async_remote_copy(
            src_ref=halves, dst_ref=halves_in.at[frm],
            send_sem=send2.at[to], recv_sem=recv2.at[frm],
            device_id=at(to, c), device_id_type=MESH,
        )

    repeat(slots - 1, lambda i: half_copy(other_slot(i), q).start())
    work[...] = rates_in[pl.ds(1, steps), 1].astype(jnp.float32).reshape(steps * 8, LANES)
    target = jnp.concatenate(
        [work[pl.ds(c * part + j, steps, stride=8), :] for j in range(part)], axis=1)
    row = lax.broadcasted_iota(jnp.int32, (steps, half), 0)
    repeat(steps - 1, lambda i: rates_copy(other_step(i), me).wait_send())
    next_copy.wait()

    panels[...] = following[...].astype(jnp.float32)

    def lay_out(i):
        target_row[:, lanes_of(i)] = panels[i // 8, pl.ds(i % 8, 1), :]

    repeat(rows * 8, lay_out)
    line = lax.broadcasted_iota(jnp.int32, (rows * pairs, steps), 0)
    step = lax.broadcasted_iota(jnp.int32, (rows * pairs, steps), 1)
    held_step = step == q * pairs + line // rows

    def chosen(k):
        hit = held_step & (lax.rem(line, rows) == row_ref[deal_ref[k]])
        return jnp.where(hit, 1.0, 0.0)

    few = slots * steps <= 512
    if few:
        choice = jnp.concatenate([chosen(k) for k in range(slots)], axis=1).astype(jnp.bfloat16)
    repeat(slots - 1, lambda i: half_copy(other_slot(i), other_slot(i)).wait_recv())

    if few:
        sums[0] = jnp.dot(choice, halves_in[...].reshape(slots * steps, half),
                          preferred_element_type=jnp.float32)
    else:
        sums[0] = jnp.zeros(sums.shape[1:], jnp.float32)

        @pl.loop(0, slots)
        def _(k):
            sums[0] = sums[0] + jnp.dot(
                chosen(k).astype(jnp.bfloat16), halves_in[k], preferred_element_type=jnp.float32)

    sum_copy = pltpu.make_async_remote_copy(
        src_ref=sums.at[0], dst_ref=sums.at[1], send_sem=send3, recv_sem=recv3,
        device_id=at(q, 1 - c), device_id_type=MESH,
    )
    sum_copy.start()
    scale = 1.0 / math.sqrt(steps)
    predicted = jnp.tanh(partial_value + halves_in[partner].astype(jnp.float32))
    mismatch = jnp.where(row < steps - 1, predicted - target, 0.0)
    signal_ref[...] = (mismatch * (1.0 - predicted * predicted) * scale).astype(jnp.bfloat16)

    repeat(slots - 1, lambda i: half_copy(other_slot(i), q).wait_send())
    sum_copy.wait()
    mine, theirs = sums[0], sums[1]
    first = c == 0
    mine = jnp.where(first, mine[:rows], mine[rows:])
    theirs = jnp.where(first, theirs[:rows], theirs[rows:])
    predicted = jnp.tanh(jnp.concatenate(
        [jnp.where(first, mine, theirs), jnp.where(first, theirs, mine)], axis=1))
    for r in range(rows):
        lanes = slice(r * pairs * half, (r + 1) * pairs * half)
        errors_ref[:, lanes] = jnp.where(
            me < steps - 1, predicted[r:r + 1] - target_row[:, lanes], 0.0).astype(jnp.bfloat16)


def gradient_kernel(signal_ref, source_ref, scale_ref, errors_ref, grads_ref, errors_out):
    term = lax.dot_general(
        signal_ref[...], source_ref[...], (((0,), (0,)), ((), ())),
        preferred_element_type=jnp.float32)
    grads_ref[0] = (term * scale_ref[...]).astype(jnp.bfloat16)
    errors_out[...] = errors_ref[...]


def shards(sizes, observed_rates, block_values, block_row, block_col, deal_list, scale_index,
           scale_table):
    regions, devs, pairs = sizes
    slots = regions * devs
    steps = slots * pairs
    neurons = observed_rates.shape[1]
    size = block_values.shape[1]
    rows = neurons // size
    bf16, f32 = jnp.bfloat16, jnp.float32
    vmem = pl.BlockSpec(memory_space=pltpu.VMEM)
    dma = pltpu.SemaphoreType.DMA
    signal, source, errors, scale = pl.pallas_call(
        functools.partial(exchange_kernel, regions, devs, pairs),
        out_shape=(
            jax.ShapeDtypeStruct((steps, size // pairs), bf16),
            jax.ShapeDtypeStruct((steps, size), bf16),
            jax.ShapeDtypeStruct((1, neurons), bf16),
            jax.ShapeDtypeStruct((1, size), f32),
        ),
        in_specs=[pl.BlockSpec(memory_space=pltpu.HBM)] * 7,
        out_specs=(vmem,) * 4,
        scratch_shapes=[
            pltpu.VMEM((rows, 8, LANES), f32),
            pltpu.VMEM((rows, 8, LANES), bf16),
            pltpu.VMEM((rows, 8, LANES), bf16),
            pltpu.VMEM((slots, 2, 8, LANES), bf16),
            pltpu.VMEM((steps + 1, 2, 8, LANES), bf16),
            pltpu.VMEM((size // pairs, size), bf16),
            pltpu.VMEM((steps * 8, LANES), f32),
            pltpu.VMEM((steps, size // pairs), bf16),
            pltpu.VMEM((slots, steps, size // pairs), bf16),
            pltpu.VMEM((2, rows * pairs, size // pairs), f32),
            pltpu.VMEM((1, neurons), f32),
            pltpu.VMEM((1, neurons), bf16),
            pltpu.SMEM(block_row.shape, jnp.int32),
            pltpu.SMEM(block_col.shape, jnp.int32),
            pltpu.SMEM(deal_list.shape, jnp.int32),
            pltpu.SMEM(scale_index.shape, jnp.int32),
            pltpu.SMEM(scale_table.shape, f32),
            dma((6,)),
            dma, dma((steps,)), dma((steps,)), dma, dma,
            dma((slots,)), dma((slots,)), dma, dma,
        ],
        compiler_params=pltpu.CompilerParams(
            collective_id=0, has_side_effects=True, vmem_limit_bytes=48 * 1024 * 1024),
        name="exchange",
    )(*(pltpu.with_memory_space_constraint(operand, pltpu.HBM) for operand in (
        observed_rates, block_values, block_row, block_col, deal_list, scale_index, scale_table)))
    grads, errors = pl.pallas_call(
        gradient_kernel,
        out_shape=(
            jax.ShapeDtypeStruct((1, size // pairs, size), bf16),
            jax.ShapeDtypeStruct((1, neurons), bf16),
        ),
        in_specs=[vmem] * 4,
        out_specs=(vmem, vmem),
        compiler_params=pltpu.CompilerParams(vmem_limit_bytes=32 * 1024 * 1024),
        name="gradient",
    )(signal, source, scale, errors)
    return (errors, grads)


def solution(mesh):
    sizes = (mesh.shape["region"], mesh.shape["dev"], mesh.shape["pair"])
    return jax.shard_map(
        functools.partial(shards, sizes),
        mesh=mesh,
        in_specs=(
            P(("parts", "region", "dev", "pair"), None),
            P(("parts", "region", "dev"), None, None),
            P("parts"),
            P("parts"),
            P("parts"),
            P(("parts", "region", "dev"), None),
            P("parts"),
        ),
        out_specs=(
            P(("parts", "region", "dev", "pair"), None),
            P(("parts", "region", "dev"), "pair", None),
        ),
        check_vma=False,
    )
```

```python
import functools
import math

import jax
import jax.numpy as jnp
from jax import lax
from jax.experimental import pallas as pl
from jax.experimental.pallas import tpu as pltpu
from jax.sharding import PartitionSpec as P

LANES = 128
MESH = pl.DeviceIdType.MESH


def repeat(count, body):
    if count <= 32:
        for i in range(count):
            body(i)
    else:
        lax.fori_loop(0, count, lambda i, carry: (body(i), carry)[1], 0)


def exchange_kernel(
    regions, devs, pairs,
    rates_hbm, values_hbm, row_hbm, col_hbm, deal_hbm, index_hbm, table_hbm,
    signal_ref, source_ref, errors_ref, scale_ref,
    panels, panels16, following, out1, rates_in, block, work, halves, halves_in, sums,
    target_row,
    rates_ref, row_ref, col_ref, deal_ref, index_ref, table_ref, small_sem,
    block_sem, send1, recv1, send_next, recv_next, send2, recv2, send3, recv3,
):
    slots = regions * devs
    steps = slots * pairs
    rows = panels.shape[0]
    half = block.shape[0]
    group = block.shape[1] // LANES
    part = half // LANES
    c = lax.axis_index("pair")
    q = lax.axis_index("region") * devs + lax.axis_index("dev")
    me = q * pairs + c

    def at(slot, core):
        return {"region": slot // devs, "dev": slot % devs, "pair": core}

    def at_step(step):
        return at(step // pairs, lax.rem(step, pairs))

    def other_step(i):
        return lax.rem(me + 1 + i, steps)

    def other_slot(i):
        return lax.rem(q + 1 + i, slots)

    def lanes_of(i):
        return pl.ds(i * LANES, LANES) if isinstance(i, int) else pl.ds(
            pl.multiple_of(i * LANES, LANES), LANES)

    smalls = [
        pltpu.make_async_copy(source, held, small_sem.at[i])
        for i, (source, held) in enumerate((
            (rates_hbm, rates_ref), (col_hbm, col_ref), (deal_hbm, deal_ref),
            (row_hbm, row_ref), (index_hbm, index_ref), (table_hbm, table_ref)))
    ]
    for copy in smalls:
        copy.start()
    load = pltpu.make_async_copy(
        values_hbm.at[0, pl.ds(pl.multiple_of(c * half, half), half)], block, block_sem)
    load.start()

    barrier = pltpu.get_barrier_semaphore()

    def greet(i):
        pl.semaphore_signal(
            barrier, inc=1, device_id=at_step(other_step(i)), device_id_type=MESH)

    repeat(steps - 1, greet)
    for copy in smalls:
        copy.wait()

    def spread(i):
        panels[i // 8, pl.ds(i % 8, 1), :] = rates_ref[:, lanes_of(i)].astype(jnp.float32)

    repeat(rows * 8, spread)
    panels16[...] = panels[...].astype(jnp.bfloat16)

    def pick(k):
        out1[k, 0] = panels[col_ref[deal_ref[k]]].astype(jnp.bfloat16)
        out1[k, 1] = panels[row_ref[deal_ref[k]]].astype(jnp.bfloat16)

    repeat(slots, pick)
    my_row = row_ref[deal_ref[q]]
    rates_in[me, 0] = panels[col_ref[deal_ref[q]]].astype(jnp.bfloat16)
    rates_in[me, 1] = panels[my_row].astype(jnp.bfloat16)
    rates_in[steps] = jnp.zeros(rates_in.shape[1:], jnp.bfloat16)
    pl.semaphore_wait(barrier, steps - 1)

    def rates_copy(to, frm):
        return pltpu.make_async_remote_copy(
            src_ref=out1.at[to // pairs], dst_ref=rates_in.at[frm],
            send_sem=send1.at[to], recv_sem=recv1.at[frm],
            device_id=at_step(to), device_id_type=MESH,
        )

    repeat(steps - 1, lambda i: rates_copy(other_step(i), me).start())
    next_copy = pltpu.make_async_remote_copy(
        src_ref=panels16, dst_ref=following, send_sem=send_next, recv_sem=recv_next,
        device_id=at_step(lax.rem(me + steps - 1, steps)), device_id_type=MESH,
    )
    next_copy.start()

    for g in range(group):
        scale_ref[:, g * LANES:(g + 1) * LANES] = jnp.full(
            (1, LANES), table_ref[index_ref[0, g]], jnp.float32)

    def same_row(k, found):
        return jnp.maximum(found, jnp.where((row_ref[deal_ref[k]] == my_row) & (k != q), k, 0))

    partner = jnp.int32(0)
    if slots <= 32:
        for k in range(slots):
            partner = same_row(k, partner)
    else:
        partner = lax.fori_loop(0, slots, same_row, partner)
    load.wait()
    chunk = 64

    @pl.loop(0, half // chunk)
    def _(i):
        piece = pl.ds(pl.multiple_of(i * chunk, chunk), chunk)
        block[piece, :] = (block[piece, :].astype(jnp.float32) * scale_ref[...]).astype(
            jnp.bfloat16)

    repeat(steps - 1, lambda i: rates_copy(other_step(i), other_step(i)).wait_recv())
    work[...] = rates_in[pl.ds(0, steps), 0].astype(jnp.float32).reshape(steps * 8, LANES)
    for j in range(group):
        source_ref[:, j * LANES:(j + 1) * LANES] = work[pl.ds(j, steps, stride=8), :].astype(
            jnp.bfloat16)
    partial_value = lax.dot_general(
        source_ref[...], block[...], (((1,), (1,)), ((), ())), preferred_element_type=jnp.float32)
    halves[...] = partial_value.astype(jnp.bfloat16)

    def half_copy(to, frm):
        return pltpu.make_async_remote_copy(
            src_ref=halves, dst_ref=halves_in.at[frm],
            send_sem=send2.at[to], recv_sem=recv2.at[frm],
            device_id=at(to, c), device_id_type=MESH,
        )

    repeat(slots - 1, lambda i: half_copy(other_slot(i), q).start())
    halves_in[q] = halves[...]
    work[...] = rates_in[pl.ds(1, steps), 1].astype(jnp.float32).reshape(steps * 8, LANES)
    target = jnp.concatenate(
        [work[pl.ds(c * part + j, steps, stride=8), :] for j in range(part)], axis=1)
    row = lax.broadcasted_iota(jnp.int32, (steps, half), 0)
    repeat(steps - 1, lambda i: rates_copy(other_step(i), me).wait_send())
    next_copy.wait()

    panels[...] = following[...].astype(jnp.float32)

    def lay_out(i):
        target_row[:, lanes_of(i)] = panels[i // 8, pl.ds(i % 8, 1), :]

    repeat(rows * 8, lay_out)
    line = lax.broadcasted_iota(jnp.int32, (rows * pairs, steps), 0)
    step = lax.broadcasted_iota(jnp.int32, (rows * pairs, steps), 1)
    held_step = step == q * pairs + line // rows

    def chosen(k):
        hit = held_step & (lax.rem(line, rows) == row_ref[deal_ref[k]])
        return jnp.where(hit, 1.0, 0.0)

    few = slots * steps <= 512
    if few:
        choice = jnp.concatenate([chosen(k) for k in range(slots)], axis=1).astype(jnp.bfloat16)
    repeat(slots - 1, lambda i: half_copy(other_slot(i), other_slot(i)).wait_recv())

    if few:
        sums[0] = jnp.dot(choice, halves_in[...].reshape(slots * steps, half),
                          preferred_element_type=jnp.float32)
    else:
        sums[0] = jnp.zeros(sums.shape[1:], jnp.float32)

        @pl.loop(0, slots)
        def _(k):
            sums[0] = sums[0] + jnp.dot(
                chosen(k).astype(jnp.bfloat16), halves_in[k], preferred_element_type=jnp.float32)

    sum_copy = pltpu.make_async_remote_copy(
        src_ref=sums.at[0], dst_ref=sums.at[1], send_sem=send3, recv_sem=recv3,
        device_id=at(q, 1 - c), device_id_type=MESH,
    )
    sum_copy.start()
    scale = 1.0 / math.sqrt(steps)
    predicted = jnp.tanh(partial_value + halves_in[partner].astype(jnp.float32))
    mismatch = jnp.where(row < steps - 1, predicted - target, 0.0)
    signal_ref[...] = (mismatch * (1.0 - predicted * predicted) * scale).astype(jnp.bfloat16)

    repeat(slots - 1, lambda i: half_copy(other_slot(i), q).wait_send())
    sum_copy.wait()
    mine, theirs = sums[0], sums[1]
    first = c == 0
    mine = jnp.where(first, mine[:rows], mine[rows:])
    theirs = jnp.where(first, theirs[:rows], theirs[rows:])
    predicted = jnp.tanh(jnp.concatenate(
        [jnp.where(first, mine, theirs), jnp.where(first, theirs, mine)], axis=1))
    for r in range(rows):
        lanes = slice(r * pairs * half, (r + 1) * pairs * half)
        errors_ref[:, lanes] = jnp.where(
            me < steps - 1, predicted[r:r + 1] - target_row[:, lanes], 0.0).astype(jnp.bfloat16)


def gradient_kernel(signal_ref, source_ref, scale_ref, errors_ref, grads_ref, errors_out):
    term = lax.dot_general(
        signal_ref[...], source_ref[...], (((0,), (0,)), ((), ())),
        preferred_element_type=jnp.float32)
    grads_ref[0] = (term * scale_ref[...]).astype(jnp.bfloat16)
    errors_out[...] = errors_ref[...]


def shards(sizes, observed_rates, block_values, block_row, block_col, deal_list, scale_index,
           scale_table):
    regions, devs, pairs = sizes
    slots = regions * devs
    steps = slots * pairs
    neurons = observed_rates.shape[1]
    size = block_values.shape[1]
    rows = neurons // size
    bf16, f32 = jnp.bfloat16, jnp.float32
    vmem = pl.BlockSpec(memory_space=pltpu.VMEM)
    dma = pltpu.SemaphoreType.DMA
    signal, source, errors, scale = pl.pallas_call(
        functools.partial(exchange_kernel, regions, devs, pairs),
        out_shape=(
            jax.ShapeDtypeStruct((steps, size // pairs), bf16),
            jax.ShapeDtypeStruct((steps, size), bf16),
            jax.ShapeDtypeStruct((1, neurons), bf16),
            jax.ShapeDtypeStruct((1, size), f32),
        ),
        in_specs=[pl.BlockSpec(memory_space=pltpu.HBM)] * 7,
        out_specs=(vmem,) * 4,
        scratch_shapes=[
            pltpu.VMEM((rows, 8, LANES), f32),
            pltpu.VMEM((rows, 8, LANES), bf16),
            pltpu.VMEM((rows, 8, LANES), bf16),
            pltpu.VMEM((slots, 2, 8, LANES), bf16),
            pltpu.VMEM((steps + 1, 2, 8, LANES), bf16),
            pltpu.VMEM((size // pairs, size), bf16),
            pltpu.VMEM((steps * 8, LANES), f32),
            pltpu.VMEM((steps, size // pairs), bf16),
            pltpu.VMEM((slots, steps, size // pairs), bf16),
            pltpu.VMEM((2, rows * pairs, size // pairs), f32),
            pltpu.VMEM((1, neurons), f32),
            pltpu.VMEM((1, neurons), bf16),
            pltpu.SMEM(block_row.shape, jnp.int32),
            pltpu.SMEM(block_col.shape, jnp.int32),
            pltpu.SMEM(deal_list.shape, jnp.int32),
            pltpu.SMEM(scale_index.shape, jnp.int32),
            pltpu.SMEM(scale_table.shape, f32),
            dma((6,)),
            dma, dma((steps,)), dma((steps,)), dma, dma,
            dma((slots,)), dma((slots,)), dma, dma,
        ],
        compiler_params=pltpu.CompilerParams(
            collective_id=0, has_side_effects=True, vmem_limit_bytes=48 * 1024 * 1024),
        name="exchange",
    )(*(pltpu.with_memory_space_constraint(operand, pltpu.HBM) for operand in (
        observed_rates, block_values, block_row, block_col, deal_list, scale_index, scale_table)))
    grads, errors = pl.pallas_call(
        gradient_kernel,
        out_shape=(
            jax.ShapeDtypeStruct((1, size // pairs, size), bf16),
            jax.ShapeDtypeStruct((1, neurons), bf16),
        ),
        in_specs=[vmem] * 4,
        out_specs=(vmem, vmem),
        compiler_params=pltpu.CompilerParams(vmem_limit_bytes=32 * 1024 * 1024),
        name="gradient",
    )(signal, source, scale, errors)
    return (errors, grads)


def solution(mesh):
    sizes = (mesh.shape["region"], mesh.shape["dev"], mesh.shape["pair"])
    return jax.shard_map(
        functools.partial(shards, sizes),
        mesh=mesh,
        in_specs=(
            P(("parts", "region", "dev", "pair"), None),
            P(("parts", "region", "dev"), None, None),
            P("parts"),
            P("parts"),
            P("parts"),
            P(("parts", "region", "dev"), None),
            P("parts"),
        ),
        out_specs=(
            P(("parts", "region", "dev", "pair"), None),
            P(("parts", "region", "dev"), "pair", None),
        ),
        check_vma=False,
    )
```
